256 devices in a mesh: fsdp: 32 (over y, x, z_hi), head: 8 (over z_lo, core).
Axes of the slice: x: 4, y: 4, z: 8 (z_hi: 2, z_lo: 4; z = z_hi * 4 + z_lo), core: 2. Of those that a mesh axis runs over, the one named last changes fastest.
Arguments:
- tokens: bfloat16 [16384, 8192], P(('fsdp', 'head')), may hold values from -6 to 6
- w_x: bfloat16 [8192, 8192], P('fsdp', 'head'), may hold values from -0.0625 to 0.0625
- w_b: bfloat16 [8192, 1024], P('fsdp', 'head'), may hold values from -0.0625 to 0.0625
- w_c: bfloat16 [8192, 1024], P('fsdp', 'head'), may hold values from -0.0625 to 0.0625
- w_dt: bfloat16 [8192, 128], P('fsdp', 'head'), may hold values from -0.0625 to 0.0625
- conv_x: float32 [4, 8192], P(None, 'head'), may hold values from -3 to 3
- conv_b: float32 [4, 1024], P(None, 'head'), may hold values from -3 to 3
- conv_c: float32 [4, 1024], P(None, 'head'), may hold values from -3 to 3
- dt_bias: float32 [128], P('head'), may hold values from -3 to 0
- decay_rate: float32 [128], P('head'), may hold values from 0.01 to 0.5
- d_skip: float32 [128], P('head'), may hold values from 0.5 to 1.5
Outputs:
- mixed: bfloat16 [16384, 8192], P(('fsdp', 'head'))
- block_states: float32 [128, 128, 64, 128], P('fsdp', 'head')
The draws below stay inside these ranges and needn't reach their ends.
All inputs are finite; a program needn't handle non-finite values.
Results may differ from the reference program's by a relative error of at most 0.0065.
Values may be sent and summed in bfloat16 or wider, within the bound.
No kernel may reach another device: no remote copies, remote signals or barrier semaphores. Data moves between devices by JAX's collectives and lax.ppermute only.
A program may use at most 128 MiB of HBM per device.

```python
import math
import jax
import jax.numpy as jnp
from jax import lax

D = 8192
HEADS = 128
HEAD_DIM = 64
STATE = 128
GROUPS = 8
CONV = 4
SPAN = 128
SEQ = 512
TOKENS = 16384
SPANS = 4
N_FSDP = 32


def block_scale(stream_key, shape, shards, least, largest):
    def one(axis_at, blocks):
        heights = jax.random.uniform(jax.random.fold_in(jax.random.fold_in(stream_key, 6), axis_at), (blocks,), jnp.float32, least / len(shards), largest / len(shards))
        return jnp.repeat(jnp.exp(heights), shape[axis_at] // blocks).reshape((-1,) + (1,) * (len(shape) - axis_at - 1))

    loudness = one(*shards[0])
    for cut in shards[1:]:
        loudness = loudness * one(*cut)
    return loudness


def centred(rng, extent, scale, bound, shards=(), kind=jnp.bfloat16):
    drawn = scale * jax.random.normal(rng, extent, jnp.float32)
    if shards:
        drawn = drawn * block_scale(rng, extent, shards, -0.22, 0.18)
    return jnp.clip(drawn, -bound, bound).astype(kind)


def setup_inputs(seed: int = 0) -> dict:
    key_list = jax.random.split(jax.random.key(seed), 12)
    return {
        "tokens": centred(key_list[0], (TOKENS, D), 1.0, 6.0, ((0, 256),)),
        "w_x": centred(key_list[1], (D, HEADS * HEAD_DIM), D ** -0.5, 0.0625, ((0, 32), (1, 8))),
        "w_b": centred(key_list[2], (D, GROUPS * STATE), D ** -0.5, 0.0625, ((0, 32), (1, 8))),
        "w_c": centred(key_list[3], (D, GROUPS * STATE), D ** -0.5, 0.0625, ((0, 32), (1, 8))),
        "w_dt": centred(key_list[4], (D, HEADS), D ** -0.5, 0.0625, ((0, 32), (1, 8))),
        "conv_x": centred(key_list[5], (CONV, HEADS * HEAD_DIM), CONV ** -0.5, 3.0, ((1, 8),), jnp.float32),
        "conv_b": centred(key_list[6], (CONV, GROUPS * STATE), CONV ** -0.5, 3.0, ((1, 8),), jnp.float32),
        "conv_c": centred(key_list[7], (CONV, GROUPS * STATE), CONV ** -0.5, 3.0, ((1, 8),), jnp.float32),
        "dt_bias": jnp.clip(-3.0 + 3.0 * jax.random.uniform(key_list[8], (HEADS,), jnp.float32) ** block_scale(key_list[8], (HEADS,), ((0, 8),), -0.2, 0.2), -3.0, 0.0),
        "decay_rate": jnp.clip(jnp.exp(math.log(0.5) - 3.912023 * jax.random.uniform(key_list[9], (HEADS,), jnp.float32) ** block_scale(key_list[9], (HEADS,), ((0, 8),), -0.2, 0.2)), 0.01, 0.5),
        "d_skip": jnp.clip(0.5 + 1.0 * jax.random.uniform(key_list[10], (HEADS,), jnp.float32) ** block_scale(key_list[10], (HEADS,), ((0, 8),), -0.2, 0.2), 0.5, 1.5),
    }


def causal_conv(values, taps):
    width = taps.shape[0]
    length = values.shape[0]
    padded = jnp.pad(values.astype(jnp.float32), ((width - 1, 0), (0, 0)))
    total = jnp.zeros((length, values.shape[1]), jnp.float32)
    for tap in range(width):
        total = total + taps[tap][None, :] * padded[tap:tap + length]
    return jax.nn.silu(total).astype(jnp.bfloat16)


def mix_sequence(projected, conv_x, conv_b, conv_c, dt_bias, decay_rate, d_skip):
    length = projected.shape[0]
    heads = dt_bias.shape[0]
    x_width = conv_x.shape[1]
    b_width = conv_b.shape[1]
    groups = b_width // STATE
    per_group = heads // groups
    blocks = length // SPAN
    xs = causal_conv(projected[:, :x_width], conv_x)
    bs = causal_conv(projected[:, x_width:x_width + b_width], conv_b)
    cs = causal_conv(projected[:, x_width + b_width:x_width + 2 * b_width], conv_c)
    step = jax.nn.softplus(projected[:, x_width + 2 * b_width:].astype(jnp.float32) + dt_bias[None, :])
    step3 = step.reshape(blocks, SPAN, heads)
    cum = jnp.cumsum(-decay_rate[None, None, :] * step3, axis=1)
    x_blocks = xs.reshape(blocks, SPAN, heads, HEAD_DIM)
    b_blocks = bs.reshape(blocks, SPAN, groups, STATE)
    c_blocks = cs.reshape(blocks, SPAN, groups, STATE)
    scores = jnp.einsum('cqgn,ckgn->cgqk', c_blocks.astype(jnp.float32), b_blocks.astype(jnp.float32))
    scores = jnp.repeat(scores, per_group, axis=1)
    cum_t = jnp.transpose(cum, (0, 2, 1))
    diff = cum_t[:, :, :, None] - cum_t[:, :, None, :]
    lower = jnp.tril(jnp.ones((SPAN, SPAN), dtype=bool))[None, None]
    decay = jnp.where(lower, jnp.exp(jnp.where(lower, diff, 0.0)), 0.0)
    step_t = jnp.transpose(step3, (0, 2, 1))[:, :, None, :]
    weights = (scores * decay * step_t).astype(jnp.bfloat16)
    output = jnp.einsum('chqk,ckhp->cqhp', weights.astype(jnp.float32), x_blocks.astype(jnp.float32))
    output = output + d_skip[None, None, :, None] * x_blocks.astype(jnp.float32)
    mixed = output.reshape(length, heads * HEAD_DIM).astype(jnp.bfloat16)
    tail = jnp.exp(cum[:, -1:, :] - cum)
    carried = (x_blocks.astype(jnp.float32) * (step3 * tail)[..., None]).astype(jnp.bfloat16)
    b_heads = jnp.repeat(b_blocks, per_group, axis=2)
    states = jnp.einsum('cqhp,cqhn->chpn', carried.astype(jnp.float32), b_heads.astype(jnp.float32))
    return mixed, states


def reference(tokens, w_x, w_b, w_c, w_dt, conv_x, conv_b, conv_c, dt_bias, decay_rate, d_skip):
    panel = jnp.concatenate([w_x, w_b, w_c, w_dt], axis=1)
    sequences = tokens.reshape(N_FSDP, SEQ, D)

    def one_sequence(rows):
        projected = jnp.dot(rows, panel, preferred_element_type=jnp.float32).astype(jnp.bfloat16)
        return mix_sequence(projected, conv_x, conv_b, conv_c, dt_bias, decay_rate, d_skip)

    mixed, states = lax.map(one_sequence, sequences)
    return mixed.reshape(TOKENS, HEADS * HEAD_DIM), states.reshape(N_FSDP * SPANS, HEADS, HEAD_DIM, STATE)
```

```python
import jax
import jax.numpy as jnp
from jax import lax
from jax.experimental import pallas as pl
from jax.experimental.pallas import tpu as pltpu
from jax.sharding import Mesh, PartitionSpec as P

HEAD_DIM = 64
STATE = 128
SPAN = 128
AXES = ("y", "x", "zh", "zl", "c")


def causal_conv(values, taps):
    width = taps.shape[0]
    length = values.shape[0]
    padded = jnp.pad(values.astype(jnp.float32), ((width - 1, 0), (0, 0)))
    total = jnp.zeros((length, values.shape[1]), jnp.float32)
    for tap in range(width):
        total = total + taps[tap][None, :] * padded[tap : tap + length]
    return jax.nn.silu(total).astype(jnp.bfloat16)


def mix_sequence(projected, conv_x, conv_b, conv_c, dt_bias, decay_rate, d_skip):
    length = projected.shape[0]
    heads = dt_bias.shape[0]
    x_width = conv_x.shape[1]
    b_width = conv_b.shape[1]
    groups = b_width // STATE
    per_group = heads // groups
    blocks = length // SPAN
    xs = causal_conv(projected[:, :x_width], conv_x)
    bs = causal_conv(projected[:, x_width : x_width + b_width], conv_b)
    cs = causal_conv(projected[:, x_width + b_width : x_width + 2 * b_width], conv_c)
    step = jax.nn.softplus(
        projected[:, x_width + 2 * b_width :].astype(jnp.float32) + dt_bias[None, :]
    )
    step3 = step.reshape(blocks, SPAN, heads)
    cum = jnp.cumsum(-decay_rate[None, None, :] * step3, axis=1)
    x_blocks = xs.reshape(blocks, SPAN, heads, HEAD_DIM)
    b_blocks = bs.reshape(blocks, SPAN, groups, STATE)
    c_blocks = cs.reshape(blocks, SPAN, groups, STATE)
    scores = jnp.einsum("cqgn,ckgn->cgqk", c_blocks, b_blocks, preferred_element_type=jnp.float32)
    scores = jnp.repeat(scores, per_group, axis=1)
    cum_t = jnp.transpose(cum, (0, 2, 1))
    diff = cum_t[:, :, :, None] - cum_t[:, :, None, :]
    lower = jnp.tril(jnp.ones((SPAN, SPAN), dtype=bool))[None, None]
    decay = jnp.where(lower, jnp.exp(jnp.where(lower, diff, 0.0)), 0.0)
    step_t = jnp.transpose(step3, (0, 2, 1))[:, :, None, :]
    weights = (scores * decay * step_t).astype(jnp.bfloat16)
    output = jnp.einsum("chqk,ckhp->cqhp", weights, x_blocks, preferred_element_type=jnp.float32)
    output = output + d_skip[None, None, :, None] * x_blocks.astype(jnp.float32)
    mixed = output.reshape(length, heads * HEAD_DIM).astype(jnp.bfloat16)
    tail = jnp.exp(cum[:, -1:, :] - cum)
    carried = (x_blocks.astype(jnp.float32) * (step3 * tail)[..., None]).astype(jnp.bfloat16)
    b_heads = jnp.repeat(b_blocks, per_group, axis=2)
    states = jnp.einsum("cqhp,cqhn->chpn", carried, b_heads, preferred_element_type=jnp.float32)
    return (mixed, states)


def reorder_kernel(place, tokens, *refs):
    outs, sems = refs[:4], refs[4]
    width = 256
    copies = []
    for part in range(4):
        for piece in range(8):
            at = part * 8 + piece
            start = pl.multiple_of(place[at] * width, width)
            copies.append(
                pltpu.make_async_copy(
                    tokens.at[:, pl.ds(start, width)],
                    outs[part].at[:, pl.ds(piece * width, width)],
                    sems.at[at],
                )
            )
    for copy in copies:
        copy.start()
    for copy in copies:
        copy.wait()


def reorder_tokens(tokens, place):
    rows = tokens.shape[0]
    return pl.pallas_call(
        reorder_kernel,
        out_shape=[jax.ShapeDtypeStruct((rows, 2048), tokens.dtype)] * 4,
        in_specs=[
            pl.BlockSpec(memory_space=pltpu.SMEM),
            pl.BlockSpec(memory_space=pl.ANY),
        ],
        out_specs=[pl.BlockSpec(memory_space=pl.ANY)] * 4,
        scratch_shapes=[pltpu.SemaphoreType.DMA((32,))],
    )(place, tokens)


def from_ahead(value, axis, distance):
    size = lax.axis_size(axis)
    return lax.ppermute(value, axis, [(i, (i - distance) % size) for i in range(size)])


def per_device(tokens, w_x, w_b, w_c, w_dt, conv_x, conv_b, conv_c, dt_bias, decay_rate, d_skip):
    y, x, zh, zl, core = (lax.axis_index(a) for a in AXES)
    panel = jnp.concatenate([w_x, w_b, w_c, w_dt], axis=1)
    twin = from_ahead(panel, "zh", 1)

    piece = jnp.arange(32, dtype=jnp.int32)
    place = (
        ((piece // 8 + y) % 4) * 8 + (((piece // 2) % 4 + x) % 4) * 2 + (piece + zh) % 2
    ).astype(jnp.int32)
    parts = reorder_tokens(tokens, place)
    rows = [parts[0]] + [from_ahead(parts[d], "y", -d) for d in (1, 2, 3)]
    own = jnp.concatenate(rows, axis=0)

    pieces = []
    for d in range(4):
        for source in (panel, twin):
            pieces.append(source if d == 0 else from_ahead(source, "x", d))
    weights = jnp.concatenate(pieces, axis=0)

    right1 = lax.ppermute(own, "zl", [(0, 1), (1, 2), (2, 3)])
    left1 = lax.ppermute(own, "zl", [(1, 0), (2, 1), (3, 2)])
    right2 = lax.ppermute(right1, "zl", [(1, 2), (2, 3)])
    left2 = lax.ppermute(left1, "zl", [(1, 0), (2, 1)])
    inner = (zl == 1) | (zl == 2)
    second = jnp.where(zl < 2, left2, right2)
    third = lax.ppermute(second, "zl", [(1, 0), (2, 3)])
    chunks = [
        own,
        jnp.where(zl == 3, right1, left1),
        jnp.where(inner, right1, second),
        jnp.where(inner, second, third),
    ]
    found = jnp.asarray([[0, 1, 2, 3], [2, 0, 1, 3], [3, 2, 0, 1], [3, 2, 1, 0]], jnp.int32)[zl]

    sums = []
    for chunk in chunks:
        other = from_ahead(chunk, "c", 1)
        both = jnp.concatenate([chunk.reshape(4, 64, 2048), other.reshape(4, 64, 2048)], axis=1)
        partial = jnp.dot(
            both.reshape(512, 2048), weights, preferred_element_type=jnp.float32
        ).reshape(4, 128, -1)
        total = partial[0]
        for d in (1, 2, 3):
            sent = partial[d].astype(jnp.bfloat16)
            total = total + from_ahead(sent, "y", d).astype(jnp.float32)
        sums.append(total.astype(jnp.bfloat16))
    stacked = jnp.stack(sums).reshape(4, 2, 64, -1)
    stacked = jnp.where(core == 0, stacked, stacked[:, ::-1])
    projected = jnp.concatenate(
        [lax.dynamic_index_in_dim(stacked, found[b], 0, keepdims=False) for b in range(4)], axis=0
    ).reshape(512, -1)

    local_mixed, states = mix_sequence(
        projected, conv_x, conv_b, conv_c, dt_bias, decay_rate, d_skip
    )
    mixed = lax.all_to_all(local_mixed, ("zl", "c"), split_axis=0, concat_axis=1, tiled=True)
    return (mixed, states)


def solution(mesh):
    fine = Mesh(mesh.devices.reshape(4, 4, 2, 4, 2), AXES)
    fsdp, head = ("y", "x", "zh"), ("zl", "c")
    in_specs = (
        P(AXES, None),
        P(fsdp, head),
        P(fsdp, head),
        P(fsdp, head),
        P(fsdp, head),
        P(None, head),
        P(None, head),
        P(None, head),
        P(head),
        P(head),
        P(head),
    )
    out_specs = (P(AXES, None), P(fsdp, head, None, None))
    return jax.shard_map(
        per_device, mesh=fine, in_specs=in_specs, out_specs=out_specs, check_vma=False
    )
```

```python
import functools

import jax
import jax.numpy as jnp
from jax import lax
from jax.experimental import pallas as pl
from jax.experimental.pallas import tpu as pltpu
from jax.sharding import Mesh, PartitionSpec as P

AXES = ("y", "x", "zh", "zl", "c")


def shifted(value, rows):
    at = lax.broadcasted_iota(jnp.int32, value.shape, 0)
    return jnp.where(at >= rows, pltpu.roll(value, rows, 0), 0.0)


def scan_block(current, before, refs, core, same, other, states):
    taps, bias, rate, skip = refs
    width = taps.shape[1]
    ext = jnp.concatenate([before[:, :width], current[:, :width]], axis=0)
    total = taps[0:1, :] * ext[13:141]
    for k in (1, 2, 3):
        total = total + taps[k : k + 1, :] * ext[13 + k : 141 + k]
    values = (total / (1.0 + jnp.exp(-total))).astype(jnp.bfloat16)
    xs, bs, cs = values[:, :1024], values[:, 1024:1152], values[:, 1152:1280]

    raw = current[:, width:] + bias[...]
    step = jnp.maximum(raw, 0.0) + jnp.log1p(jnp.exp(-jnp.abs(raw)))
    cum = -rate[...] * step
    for rows in (1, 2, 4, 8, 16, 32, 64):
        cum = cum + shifted(cum, rows)
    cum_t, step_t = cum.T, step.T
    factor = step * jnp.exp(cum[127:128, :] - cum)
    scores = lax.dot_general(cs, bs, (((1,), (1,)), ((), ())), preferred_element_type=jnp.float32)
    lower = lax.broadcasted_iota(jnp.int32, (128, 128), 0) >= lax.broadcasted_iota(
        jnp.int32, (128, 128), 1
    )
    left = lax.broadcasted_iota(jnp.int32, (128, 128), 1) < 64
    for pair in range(8):
        lanes = slice(128 * pair, 128 * pair + 128)
        x_pair = xs[:, lanes]
        wide = x_pair.astype(jnp.float32)
        outs = []
        for h in (2 * pair, 2 * pair + 1):
            diff = cum[:, h : h + 1] - cum_t[h : h + 1, :]
            decay = jnp.exp(jnp.where(lower, diff, -1e30))
            weights = (scores * decay * step_t[h : h + 1, :]).astype(jnp.bfloat16)
            outs.append(jnp.dot(weights, x_pair, preferred_element_type=jnp.float32))
        out = jnp.where(left, outs[0], outs[1]) + skip[:, lanes] * wide
        out = out.astype(jnp.bfloat16)
        top, bottom = out[:64], out[64:]
        same[:, lanes] = jnp.where(core == 0, top, bottom)
        other[:, lanes] = jnp.where(core == 0, bottom, top)
        column = jnp.where(
            left, factor[:, 2 * pair : 2 * pair + 1], factor[:, 2 * pair + 1 : 2 * pair + 2]
        )
        carried = (wide * column).astype(jnp.bfloat16)
        state = lax.dot_general(
            carried, bs, (((0,), (0,)), ((), ())), preferred_element_type=jnp.float32
        )
        states[2 * pair] = state[:64]
        states[2 * pair + 1] = state[64:]


def scan_kernel(late, place, *refs):
    core, zl = place[0], place[1]
    if late:
        near, edge, swapped, came, *refs = refs
        refs = refs[:4] + refs[5:]
    else:
        own, near, edge, swapped, *refs = refs
    params, outs = refs[:4], refs[4:]
    pieces, states, scratch, sems = outs[:4], outs[4], outs[5], outs[6]

    def whole(ref):
        return ref[...].astype(jnp.float32)

    def tail(value):
        return value[112:128]

    ahead = jnp.where(zl == 3, whole(swapped), whole(near))
    behind = jnp.where(zl == 0, whole(swapped), whole(edge))
    if late:
        beyond = jnp.sum(came[...].astype(jnp.float32), axis=0)
        beyond = beyond.astype(jnp.bfloat16).astype(jnp.float32)
        work = [
            (behind, jnp.where(zl == 1, 0.0, tail(beyond)), lax.rem(zl + 3, 4)),
            (beyond, jnp.where(zl == 2, 0.0, tail(ahead)), lax.rem(zl + 2, 4)),
        ]
    else:
        mine = whole(own)
        work = [
            (mine, jnp.where(zl == 0, 0.0, tail(behind)), zl),
            (ahead, jnp.where(zl == 3, 0.0, tail(mine)), lax.rem(zl + 1, 4)),
        ]
    copies = []
    for k, (current, before, block) in enumerate(work):
        scan_block(current, before, params, core, pieces[2 * k], pieces[2 * k + 1], scratch.at[k])
        copies.append(pltpu.make_async_copy(scratch.at[k], states.at[block], sems.at[k]))
        copies[-1].start()
    for copy in copies:
        copy.wait()


def scan(place, sums, params, states=None):
    whole = pl.BlockSpec(memory_space=pltpu.VMEM)
    late = states is not None
    operands = [place, *sums, *params] + ([states] if late else [])
    in_specs = [pl.BlockSpec(memory_space=pltpu.SMEM)] + [whole] * (len(sums) + len(params))
    in_specs += [pl.BlockSpec(memory_space=pl.ANY)] if late else []
    return pl.pallas_call(
        functools.partial(scan_kernel, late),
        out_shape=[jax.ShapeDtypeStruct((64, 1024), jnp.bfloat16)] * 4
        + [jax.ShapeDtypeStruct((4, 16, 64, 128), jnp.float32)],
        in_specs=in_specs,
        out_specs=[whole] * 4 + [pl.BlockSpec(memory_space=pl.ANY)],
        scratch_shapes=[
            pltpu.VMEM((2, 16, 64, 128), jnp.float32),
            pltpu.SemaphoreType.DMA((2,)),
        ],
        input_output_aliases={len(operands) - 1: 4} if late else {},
        compiler_params=pltpu.CompilerParams(vmem_limit_bytes=48 << 20),
        cost_estimate=pl.CostEstimate(flops=1 << 20, bytes_accessed=1 << 16, transcendentals=0),
    )(*operands)


def assemble_kernel(place, *refs):
    pieces, out = refs[:-1], refs[-1]
    for k, piece in enumerate(pieces):
        out[:, pl.ds(pl.multiple_of(place[k] * 1024, 1024), 1024)] = piece[...]


def assemble(place, pieces):
    whole = pl.BlockSpec(memory_space=pltpu.VMEM)
    return pl.pallas_call(
        assemble_kernel,
        out_shape=jax.ShapeDtypeStruct((64, 8192), jnp.bfloat16),
        in_specs=[pl.BlockSpec(memory_space=pltpu.SMEM)] + [whole] * 8,
        out_specs=whole,
        compiler_params=pltpu.CompilerParams(vmem_limit_bytes=16 << 20),
    )(place, *pieces)


def reorder_kernel(place, tokens, out):
    width = 256
    for part in range(4):
        for piece in range(8):
            start = pl.multiple_of(place[part * 8 + piece] * width, width)
            out[part, :, piece * width : (piece + 1) * width] = tokens[:, pl.ds(start, width)]


def reorder_tokens(tokens, place):
    rows = tokens.shape[0]
    whole = pl.BlockSpec(memory_space=pltpu.VMEM)
    return pl.pallas_call(
        reorder_kernel,
        out_shape=jax.ShapeDtypeStruct((4, rows, 2048), tokens.dtype),
        in_specs=[pl.BlockSpec(memory_space=pltpu.SMEM), whole],
        out_specs=whole,
        compiler_params=pltpu.CompilerParams(vmem_limit_bytes=16 << 20),
    )(place, tokens)


TILE = 256


def project_kernel(pairs, start, place, *refs):
    chunks, refs = refs[: 2 * pairs], refs[2 * pairs :]
    panels, out = refs[:-1], refs[-1]
    tile = pl.program_id(0)
    core, zh = place[0], place[2]

    def work(group, paired):
        values = [ref[...] for ref in group]
        ordered = [jnp.where(zh == 0, a, b) for a, b in zip(values[:2], values[2:])]
        ordered += [jnp.where(zh == 0, b, a) for a, b in zip(values[:2], values[2:])]
        values = ordered
        if not paired:
            values = [v[h : h + 256] for f in (0, 2) for h in (0, 256) for v in values[f : f + 2]]
        rhs = jnp.concatenate(values, axis=0)
        for p in range(pairs):
            lhs = jnp.concatenate([chunks[2 * p][...], chunks[2 * p + 1][...]], axis=0)
            partial = jnp.dot(lhs, rhs, preferred_element_type=jnp.float32).astype(out.dtype)
            for half, at in ((0, core), (256, 1 - core)):
                rows = pl.ds(pl.multiple_of(p * 128 + at * 64, 64), 64)
                for d in range(4):
                    low = half + 64 * d
                    out[d, rows, :] = partial[low : low + 64]

    pl.when(tile < start)(lambda: work(panels[:4], True))
    pl.when(tile >= start)(lambda: work(panels[4:], False))


def project(place, chunks, panels):
    pairs = len(chunks) // 2
    widths = [panel.shape[1] for panel in panels[::4]]
    counts = [pl.cdiv(width, TILE) for width in widths]
    whole = pl.BlockSpec((256, 2048), lambda j: (0, 0))
    first = pl.BlockSpec((512, TILE), lambda j: (0, jnp.minimum(j, counts[0] - 1)))
    last = pl.BlockSpec((512, TILE), lambda j: (0, jnp.maximum(j - counts[0], 0)))
    return pl.pallas_call(
        functools.partial(project_kernel, pairs, counts[0]),
        grid=(sum(counts),),
        out_shape=jax.ShapeDtypeStruct((4, 128 * pairs, sum(widths)), jnp.bfloat16),
        in_specs=[pl.BlockSpec(memory_space=pltpu.SMEM)]
        + [whole] * len(chunks) + [first] * 4 + [last] * 4,
        out_specs=pl.BlockSpec((4, 128 * pairs, TILE), lambda j: (0, 0, j)),
        compiler_params=pltpu.CompilerParams(vmem_limit_bytes=60 << 20),
        cost_estimate=pl.CostEstimate(flops=1 << 20, bytes_accessed=1 << 16, transcendentals=0),
    )(place, *chunks, *panels)


def from_ahead(value, axis, distance):
    size = lax.axis_size(axis)
    return lax.ppermute(value, axis, [(i, (i - distance) % size) for i in range(size)])


def after(values, *others):
    flat, tree = jax.tree.flatten(values)
    held = lax.optimization_barrier(tuple(flat) + tuple(jax.tree.leaves(others)))
    return jax.tree.unflatten(tree, held[: len(flat)])


NEXT = [(i, i ^ 1) for i in range(4)]
MIRROR = [(i, 3 - i) for i in range(4)]


def gather_x(panel, pairings):
    both = jnp.concatenate([panel, lax.ppermute(panel, "x", pairings[0])], axis=0)
    return [both, lax.ppermute(both, "x", pairings[1])]


def exchange(partial):
    return lax.all_to_all(partial, "y", split_axis=0, concat_axis=0, tiled=True)


def add_up(came):
    return jnp.sum(came.astype(jnp.float32), axis=0).astype(jnp.bfloat16)


def per_device(tokens, w_x, w_b, w_c, w_dt, conv_x, conv_b, conv_c, dt_bias, decay_rate, d_skip):
    y, x, zh, zl, core = (lax.axis_index(a) for a in AXES)
    split = 768
    panel = jnp.concatenate([w_x, w_b, w_c, jnp.pad(w_dt, ((0, 0), (0, 112)))], axis=1)
    twin = from_ahead(panel, "zh", 1)
    near_a = gather_x(panel[:, :split], (NEXT, MIRROR))
    near_b = gather_x(panel[:, split:], (MIRROR, NEXT))

    sources = jnp.stack([x, x ^ 1, 3 - x, 3 - (x ^ 1)])
    order = (
        jnp.arange(4)[:, None, None] * 8
        + jnp.arange(2)[None, :, None]
        + sources[None, None, :] * 2
    ).astype(jnp.int32).reshape(32)
    parts = reorder_tokens(after(tokens, panel), order)
    own = lax.all_to_all(parts, "y", split_axis=0, concat_axis=0, tiled=True).reshape(256, 2048)
    own_other = from_ahead(own, "c", 1)

    line = ("zh", "zl")
    own_sent, twin = after((own, twin), near_a, near_b)
    right1 = lax.ppermute(own_sent, line, [(i, (i + 1) % 8) for i in range(8)])
    left1 = lax.ppermute(own_sent, line, [(i, (i - 1) % 8) for i in range(8)])
    panels = near_a + gather_x(twin[:, :split], (NEXT, MIRROR))
    panels += near_b + gather_x(twin[:, split:], (MIRROR, NEXT))

    place = jnp.stack([core, zl, zh]).astype(jnp.int32)
    partial = project(place, [own, own_other], panels)
    came_own = exchange(partial)

    right2 = lax.ppermute(right1, line, [(1, 2), (2, 3), (5, 6), (6, 7)])
    left2 = lax.ppermute(left1, line, [(1, 0), (2, 1), (5, 4), (6, 5)])
    sides = [left1, from_ahead(left1, "c", 1), right1, from_ahead(right1, "c", 1)]
    partial = project(place, after(sides, partial), panels)
    came_sides = exchange(partial)

    second = jnp.where(zl < 2, left2, right2)
    pair = after([second, from_ahead(second, "c", 1)], partial)
    partial = project(place, pair, panels)
    came_own, came_sides = after((came_own, came_sides), partial)
    came_second = exchange(partial)

    params = [
        jnp.concatenate([conv_x, conv_b, conv_c], axis=1),
        jnp.pad(dt_bias, (0, 112))[None],
        jnp.pad(decay_rate, (0, 112))[None],
        jnp.repeat(d_skip, 64)[None],
    ]
    own_sum, both = add_up(came_own), add_up(came_sides)
    left, right = both[:128], both[128:]
    swapped = lax.ppermute(
        jnp.where(zl == 3, left, right), line, [(i, (i + 4) % 8) for i in (0, 3, 4, 7)]
    )
    *early, states = scan(place, [own_sum, left, right, swapped], params)
    *last, states = scan(place, [left, right, swapped, came_second], params, states)
    heads = ("zl", "c")

    def to(piece, distance, flip):
        pairs = [
            (2 * z + c, 2 * ((z + distance) % 4) + (c ^ flip)) for z in range(4) for c in range(2)
        ]
        return lax.ppermute(piece, heads, pairs)

    pieces = [
        early[0], to(early[1], 0, 1), to(early[2], 1, 0), to(early[3], 1, 1),
        to(last[0], 3, 0), to(last[1], 3, 1), to(last[2], 2, 0), to(last[3], 2, 1),
    ]
    origin = zl + jnp.asarray([0, 0, 3, 3, 1, 1, 2, 2])
    columns = (origin % 4) * 2 + (core + jnp.asarray([0, 1] * 4)) % 2
    return (assemble(columns.astype(jnp.int32), pieces), states)


def solution(mesh):
    fine = Mesh(mesh.devices.reshape(4, 4, 2, 4, 2), AXES)
    fsdp, head = ("y", "x", "zh"), ("zl", "c")
    in_specs = (
        P(AXES, None),
        P(fsdp, head),
        P(fsdp, head),
        P(fsdp, head),
        P(fsdp, head),
        P(None, head),
        P(None, head),
        P(None, head),
        P(head),
        P(head),
        P(head),
    )
    out_specs = (P(AXES, None), P(fsdp, head, None, None))
    return jax.shard_map(
        per_device, mesh=fine, in_specs=in_specs, out_specs=out_specs, check_vma=False
    )
```

```python
import functools

import jax
import jax.numpy as jnp
from jax import lax
from jax.experimental import pallas as pl
from jax.experimental.pallas import tpu as pltpu
from jax.sharding import Mesh, PartitionSpec as P

AXES = ("y", "x", "zh", "zl", "c")


def shifted(value, rows):
    at = lax.broadcasted_iota(jnp.int32, value.shape, 0)
    return jnp.where(at >= rows, pltpu.roll(value, rows, 0), 0.0)


def scan_block(current, before, refs, core, mixed, states):
    taps, bias, rate, skip = refs
    width = taps.shape[1]
    ext = jnp.concatenate([before[:, :width], current[:, :width]], axis=0)
    total = taps[0:1, :] * ext[13:141]
    for k in (1, 2, 3):
        total = total + taps[k : k + 1, :] * ext[13 + k : 141 + k]
    values = (total / (1.0 + jnp.exp(-total))).astype(jnp.bfloat16)
    xs, bs, cs = values[:, :1024], values[:, 1024:1152], values[:, 1152:1280]

    raw = current[:, width:] + bias[...]
    step = jnp.maximum(raw, 0.0) + jnp.log1p(jnp.exp(-jnp.abs(raw)))
    cum = -rate[...] * step
    for rows in (1, 2, 4, 8, 16, 32, 64):
        cum = cum + shifted(cum, rows)
    cum_t, step_t = cum.T, step.T
    factor = step * jnp.exp(cum[127:128, :] - cum)
    scores = lax.dot_general(cs, bs, (((1,), (1,)), ((), ())), preferred_element_type=jnp.float32)
    lower = lax.broadcasted_iota(jnp.int32, (128, 128), 0) >= lax.broadcasted_iota(
        jnp.int32, (128, 128), 1
    )
    left = lax.broadcasted_iota(jnp.int32, (128, 128), 1) < 64
    for pair in range(8):
        lanes = slice(128 * pair, 128 * pair + 128)
        x_pair = xs[:, lanes]
        wide = x_pair.astype(jnp.float32)
        outs = []
        for h in (2 * pair, 2 * pair + 1):
            diff = cum[:, h : h + 1] - cum_t[h : h + 1, :]
            decay = jnp.exp(jnp.where(lower, diff, -1e30))
            weights = (scores * decay * step_t[h : h + 1, :]).astype(jnp.bfloat16)
            outs.append(jnp.dot(weights, x_pair, preferred_element_type=jnp.float32))
        out = jnp.where(left, outs[0], outs[1]) + skip[:, lanes] * wide
        out = out.astype(jnp.bfloat16)
        top, bottom = out[:64], out[64:]
        mixed[:64, lanes] = jnp.where(core == 0, top, bottom)
        mixed[64:, lanes] = jnp.where(core == 0, bottom, top)
        column = jnp.where(
            left, factor[:, 2 * pair : 2 * pair + 1], factor[:, 2 * pair + 1 : 2 * pair + 2]
        )
        carried = (wide * column).astype(jnp.bfloat16)
        state = lax.dot_general(
            carried, bs, (((0,), (0,)), ((), ())), preferred_element_type=jnp.float32
        )
        states[2 * pair] = state[:64]
        states[2 * pair + 1] = state[64:]


def scan_kernel(late, place, *refs):
    core, zl = place[0], place[1]
    sums, swapped, came, *refs = refs
    if late:
        refs = refs[:4] + refs[5:]
    params, outs = refs[:4], refs[4:]
    mixed, states, scratch, sems = outs[:2], outs[2], outs[3], outs[4]

    def whole(ref):
        return ref[...].astype(jnp.float32)

    def tail(value):
        return value[112:128]

    ahead = jnp.where(zl == 3, whole(swapped), sums[:128].astype(jnp.float32))
    behind = jnp.where(zl == 0, whole(swapped), sums[128:].astype(jnp.float32))
    total = jnp.sum(whole(came), axis=0).astype(jnp.bfloat16).astype(jnp.float32)
    if late:
        beyond = total
        work = [
            (behind, jnp.where(zl == 1, 0.0, tail(beyond)), lax.rem(zl + 3, 4)),
            (beyond, jnp.where(zl == 2, 0.0, tail(ahead)), lax.rem(zl + 2, 4)),
        ]
    else:
        mine = total
        work = [
            (mine, jnp.where(zl == 0, 0.0, tail(behind)), zl),
            (ahead, jnp.where(zl == 3, 0.0, tail(mine)), lax.rem(zl + 1, 4)),
        ]
    copies = []
    for k, (current, before, block) in enumerate(work):
        scan_block(current, before, params, core, mixed[k], scratch.at[k])
        copies.append(pltpu.make_async_copy(scratch.at[k], states.at[block], sems.at[k]))
        copies[-1].start()
    for copy in copies:
        copy.wait()


def scan(place, sums, params, states=None):
    whole = pl.BlockSpec(memory_space=pltpu.VMEM)
    late = states is not None
    operands = [place, *sums, *params] + ([states] if late else [])
    in_specs = [pl.BlockSpec(memory_space=pltpu.SMEM)] + [whole] * (len(sums) + len(params))
    in_specs += [pl.BlockSpec(memory_space=pl.ANY)] if late else []
    return pl.pallas_call(
        functools.partial(scan_kernel, late),
        out_shape=[jax.ShapeDtypeStruct((128, 1024), jnp.bfloat16)] * 2
        + [jax.ShapeDtypeStruct((4, 16, 64, 128), jnp.float32)],
        in_specs=in_specs,
        out_specs=[whole] * 2 + [pl.BlockSpec(memory_space=pl.ANY)],
        scratch_shapes=[
            pltpu.VMEM((2, 16, 64, 128), jnp.float32),
            pltpu.SemaphoreType.DMA((2,)),
        ],
        input_output_aliases={len(operands) - 1: 2} if late else {},
        compiler_params=pltpu.CompilerParams(vmem_limit_bytes=48 << 20),
        cost_estimate=pl.CostEstimate(flops=1 << 20, bytes_accessed=1 << 16, transcendentals=0),
    )(*operands)


def assemble_kernel(place, *refs):
    blocks, other, out = refs[:4], refs[4], refs[5]
    pieces = [block[:64] for block in blocks] + [other[64 * k : 64 * k + 64] for k in range(4)]
    for k, piece in enumerate(pieces):
        out[:, pl.ds(pl.multiple_of(place[k] * 1024, 1024), 1024)] = piece


def assemble(place, pieces):
    whole = pl.BlockSpec(memory_space=pltpu.VMEM)
    return pl.pallas_call(
        assemble_kernel,
        out_shape=jax.ShapeDtypeStruct((64, 8192), jnp.bfloat16),
        in_specs=[pl.BlockSpec(memory_space=pltpu.SMEM)] + [whole] * 5,
        out_specs=whole,
        compiler_params=pltpu.CompilerParams(vmem_limit_bytes=16 << 20),
    )(place, *pieces)


def reorder_kernel(place, tokens, *outs):
    width = 256
    for part in range(4):
        for piece in range(8):
            start = pl.multiple_of(place[part * 8 + piece] * width, width)
            outs[part][:, piece * width : (piece + 1) * width] = tokens[:, pl.ds(start, width)]


def reorder_tokens(tokens, place):
    rows = tokens.shape[0]
    whole = pl.BlockSpec(memory_space=pltpu.VMEM)
    return pl.pallas_call(
        reorder_kernel,
        out_shape=[jax.ShapeDtypeStruct((rows, 2048), tokens.dtype)] * 4,
        in_specs=[pl.BlockSpec(memory_space=pltpu.SMEM), whole],
        out_specs=[whole] * 4,
        compiler_params=pltpu.CompilerParams(vmem_limit_bytes=16 << 20),
    )(place, tokens)


TILE = 768


def project_kernel(pairs, start, place, *refs):
    chunks, refs = refs[: 2 * pairs], refs[2 * pairs :]
    near, far, out = refs[:4], refs[4:8], refs[8]
    tile = pl.program_id(0)
    core, zh, y = place[0], place[2], place[3]

    def work(group, paired):
        mine = jnp.concatenate([ref[...] for ref in near], axis=0)
        values = [ref[...] for ref in group]
        if not paired:
            values = [value[h : h + 256] for h in (0, 256) for value in values]
        twin = jnp.concatenate(values, axis=0)
        rhs = jnp.concatenate(
            [jnp.where(zh == 0, mine, twin), jnp.where(zh == 0, twin, mine)], axis=0
        )
        for p in range(pairs):
            lhs = jnp.concatenate([chunks[2 * p][...], chunks[2 * p + 1][...]], axis=0)
            partial = jnp.dot(lhs, rhs, preferred_element_type=jnp.float32)
            for half, at in ((0, core), (256, 1 - core)):
                rows = pl.ds(pl.multiple_of(p * 128 + at * 64, 64), 64)
                for d in range(4):
                    low = half + 64 * d
                    out[y ^ d, rows, :] = partial[low : low + 64].astype(jnp.bfloat16)

    pl.when(tile < start)(lambda: work(far[:2], True))
    pl.when(tile >= start)(lambda: work(far[2:], False))


def project(place, chunks, panels):
    pairs = len(chunks) // 2
    widths = [panels[4].shape[1], panels[6].shape[1]]
    counts = [pl.cdiv(width, TILE) for width in widths]
    whole = pl.BlockSpec((256, 2048), lambda j: (0, 0))
    near = pl.BlockSpec((256, TILE), lambda j: (0, j))
    first = pl.BlockSpec((512, TILE), lambda j: (0, jnp.minimum(j, counts[0] - 1)))
    last = pl.BlockSpec((512, TILE), lambda j: (0, jnp.maximum(j - counts[0], 0)))
    return pl.pallas_call(
        functools.partial(project_kernel, pairs, counts[0]),
        grid=(sum(counts),),
        out_shape=jax.ShapeDtypeStruct((4, 128 * pairs, sum(widths)), jnp.bfloat16),
        in_specs=[pl.BlockSpec(memory_space=pltpu.SMEM)]
        + [whole] * len(chunks) + [near] * 4 + [first] * 2 + [last] * 2,
        out_specs=pl.BlockSpec((4, 128 * pairs, TILE), lambda j: (0, 0, j)),
        compiler_params=pltpu.CompilerParams(vmem_limit_bytes=60 << 20),
        cost_estimate=pl.CostEstimate(flops=1 << 20, bytes_accessed=1 << 16, transcendentals=0),
    )(place, *chunks, *panels)


def after(values, *others):
    flat, tree = jax.tree.flatten(values)
    held = lax.optimization_barrier(tuple(flat) + tuple(jax.tree.leaves(others)))
    return jax.tree.unflatten(tree, held[: len(flat)])


def swap(value, axis, distance):
    size = lax.axis_size(axis)
    return lax.ppermute(value, axis, [(i, i ^ distance) for i in range(size)])


def gather_x(panel, first, second, *others):
    both = jnp.concatenate([panel, swap(panel, "x", first)], axis=0)
    return [both, swap(after(both, *others), "x", second)]


def exchange(parts):
    return lax.all_to_all(parts, "y", split_axis=0, concat_axis=0, tiled=True)


def add_up(came):
    return jnp.sum(came.astype(jnp.float32), axis=0).astype(jnp.bfloat16)


def per_device(tokens, w_x, w_b, w_c, w_dt, conv_x, conv_b, conv_c, dt_bias, decay_rate, d_skip):
    y, x, zh, zl, core = (lax.axis_index(a) for a in AXES)
    split = TILE
    panel = jnp.concatenate([w_x, w_b, w_c, jnp.pad(w_dt, ((0, 0), (0, 112)))], axis=1)
    twin = swap(panel, "zh", 1)
    near = [panel] + [swap(panel, "x", d) for d in (1, 3, 2)]

    sources = x ^ jnp.asarray([0, 1, 3, 2])
    order = (
        (jnp.arange(4) ^ y)[:, None, None] * 8
        + jnp.arange(2)[None, :, None]
        + sources[None, None, :] * 2
    ).astype(jnp.int32).reshape(32)
    parts = reorder_tokens(after(tokens, panel), order)
    rows = [parts[0]] + [swap(parts[d], "y", d) for d in (1, 2, 3)]
    own = jnp.concatenate(rows, axis=0)
    own_other = swap(own, "c", 1)

    line = ("zh", "zl")
    own_sent, twin = after((own, twin), near)
    right1 = lax.ppermute(own_sent, line, [(i, (i + 1) % 8) for i in range(8)])
    left1 = lax.ppermute(own_sent, line, [(i, (i - 1) % 8) for i in range(8)])
    panels = near + gather_x(twin[:, :split], 1, 3)
    panels += gather_x(twin[:, split:], 3, 1)

    place = jnp.stack([core, zl, zh, y]).astype(jnp.int32)
    left1, right1 = after((left1, right1), panels)
    sides = [left1, swap(left1, "c", 1), right1, swap(right1, "c", 1)]
    parts = project(place, [own, own_other], panels)
    came_own = exchange(parts)
    parts = project(place, after(sides, parts), panels)
    came_sides = exchange(parts)

    left1, right1 = after((left1, right1), parts)
    right2 = lax.ppermute(right1, line, [(1, 2), (2, 3), (5, 6), (6, 7)])
    left2 = lax.ppermute(left1, line, [(1, 0), (2, 1), (5, 4), (6, 5)])
    second = jnp.where(zl < 2, left2, right2)
    pair = after([second, swap(second, "c", 1)], parts)
    parts = project(place, pair, panels)
    came_own, came_sides = after((came_own, came_sides), parts)
    came_second = exchange(parts)

    params = [
        jnp.concatenate([conv_x, conv_b, conv_c], axis=1),
        jnp.pad(dt_bias, (0, 112))[None],
        jnp.pad(decay_rate, (0, 112))[None],
        jnp.repeat(d_skip, 64)[None],
    ]
    sums = add_up(came_sides)
    swapped = lax.ppermute(
        jnp.where(zl == 3, sums[:128], sums[128:]), line, [(i, (i + 4) % 8) for i in (0, 3, 4, 7)]
    )
    *early, states = scan(place, [sums, swapped, came_own], params)
    def to(block, distance):
        return lax.ppermute(block, "zl", [(z, (z + distance) % 4) for z in range(4)])

    ahead = to(early[1], 1)
    came_second, ahead = after((came_second, ahead))
    *last, states = scan(place, [sums, swapped, came_second], params, states)
    blocks = [early[0], ahead, to(last[0], 3), to(last[1], 2)]
    other = swap(jnp.concatenate([block[64:] for block in blocks], axis=0), "c", 1)
    origin = (zl + jnp.asarray([0, 3, 1, 2])) % 4
    columns = jnp.concatenate([origin * 2 + core, origin * 2 + 1 - core])
    return (assemble(columns.astype(jnp.int32), blocks + [other]), states)


def solution(mesh):
    fine = Mesh(mesh.devices.reshape(4, 4, 2, 4, 2), AXES)
    fsdp, head = ("y", "x", "zh"), ("zl", "c")
    in_specs = (
        P(AXES, None),
        P(fsdp, head),
        P(fsdp, head),
        P(fsdp, head),
        P(fsdp, head),
        P(None, head),
        P(None, head),
        P(None, head),
        P(head),
        P(head),
        P(head),
    )
    out_specs = (P(AXES, None), P(fsdp, head, None, None))
    return jax.shard_map(
        per_device, mesh=fine, in_specs=in_specs, out_specs=out_specs, check_vma=False
    )
```

```python
import functools

import jax
import jax.numpy as jnp
from jax import lax
from jax.experimental import pallas as pl
from jax.experimental.pallas import tpu as pltpu
from jax.sharding import Mesh, PartitionSpec as P

AXES = ("y", "x", "zh", "zl", "c")


def shifted(value, rows):
    at = lax.broadcasted_iota(jnp.int32, value.shape, 0)
    return jnp.where(at >= rows, pltpu.roll(value, rows, 0), 0.0)


def scan_block(current, before, refs, core, same, other, states):
    taps, bias, rate, skip = refs
    width = taps.shape[1]
    ext = jnp.concatenate([before[:, :width], current[:, :width]], axis=0)
    total = taps[0:1, :] * ext[13:141]
    for k in (1, 2, 3):
        total = total + taps[k : k + 1, :] * ext[13 + k : 141 + k]
    values = (total / (1.0 + jnp.exp(-total))).astype(jnp.bfloat16)
    xs, bs, cs = values[:, :1024], values[:, 1024:1152], values[:, 1152:1280]

    raw = current[:, width:] + bias[...]
    step = jnp.maximum(raw, 0.0) + jnp.log1p(jnp.exp(-jnp.abs(raw)))
    cum = -rate[...] * step
    for rows in (1, 2, 4, 8, 16, 32, 64):
        cum = cum + shifted(cum, rows)
    cum_t, step_t = cum.T, step.T
    factor = step * jnp.exp(cum[127:128, :] - cum)
    scores = lax.dot_general(cs, bs, (((1,), (1,)), ((), ())), preferred_element_type=jnp.float32)
    lower = lax.broadcasted_iota(jnp.int32, (128, 128), 0) >= lax.broadcasted_iota(
        jnp.int32, (128, 128), 1
    )
    left = lax.broadcasted_iota(jnp.int32, (128, 128), 1) < 64
    for pair in range(8):
        lanes = slice(128 * pair, 128 * pair + 128)
        x_pair = xs[:, lanes]
        wide = x_pair.astype(jnp.float32)
        outs = []
        for h in (2 * pair, 2 * pair + 1):
            diff = cum[:, h : h + 1] - cum_t[h : h + 1, :]
            decay = jnp.exp(jnp.where(lower, diff, -1e30))
            weights = (scores * decay * step_t[h : h + 1, :]).astype(jnp.bfloat16)
            outs.append(jnp.dot(weights, x_pair, preferred_element_type=jnp.float32))
        out = jnp.where(left, outs[0], outs[1]) + skip[:, lanes] * wide
        out = out.astype(jnp.bfloat16)
        top, bottom = out[:64], out[64:]
        same[:, lanes] = jnp.where(core == 0, top, bottom)
        other[:, lanes] = jnp.where(core == 0, bottom, top)
        column = jnp.where(
            left, factor[:, 2 * pair : 2 * pair + 1], factor[:, 2 * pair + 1 : 2 * pair + 2]
        )
        carried = (wide * column).astype(jnp.bfloat16)
        state = lax.dot_general(
            carried, bs, (((0,), (0,)), ((), ())), preferred_element_type=jnp.float32
        )
        states[2 * pair] = state[:64]
        states[2 * pair + 1] = state[64:]


def scan_kernel(late, place, *refs):
    core, zl = place[0], place[1]
    sums, came, *refs = refs
    if late:
        swapped, *refs = refs
        refs = refs[:4] + refs[5:]
    params, (*pieces, states, scratch, sems) = refs[:4], refs[4:]

    def whole(ref):
        return ref[...].astype(jnp.float32)

    def tail(value):
        return value[112:128]

    ahead, behind = (sums[k : k + 128].astype(jnp.float32) for k in (0, 128))
    total = jnp.sum(whole(came), axis=0).astype(jnp.bfloat16).astype(jnp.float32)
    always = zl >= 0
    if late:
        first = whole(swapped)
        ahead = jnp.where(zl == 3, first, ahead)
        behind = jnp.where(zl == 0, first, behind)
        work = [
            (zl == 3, first, jnp.zeros_like(tail(first)), 0),
            (always, total, jnp.where(zl == 2, 0.0, tail(ahead)), lax.rem(zl + 2, 4)),
            (always, behind, jnp.where(zl == 1, 0.0, tail(total)), lax.rem(zl + 3, 4)),
        ]
    else:
        work = [
            (always, total, jnp.where(zl == 0, 0.0, tail(behind)), zl),
            (zl < 3, ahead, tail(total), lax.rem(zl + 1, 4)),
        ]

    def copy(k, block):
        return pltpu.make_async_copy(scratch.at[k], states.at[block], sems.at[k])

    for k, (needed, current, before, block) in enumerate(work):
        @pl.when(needed)
        def _(k=k, current=current, before=before, block=block):
            same, other = pieces[2 * k], pieces[2 * k + 1]
            scan_block(current, before, params, core, same, other, scratch.at[k])
            copy(k, block).start()

    for k, (needed, _, _, block) in enumerate(work):
        pl.when(needed)(lambda k=k, block=block: copy(k, block).wait())


def scan(place, sums, params, states=None):
    whole = pl.BlockSpec(memory_space=pltpu.VMEM)
    late = states is not None
    blocks = 3 if late else 2
    operands = [place, *sums, *params] + ([states] if late else [])
    in_specs = [pl.BlockSpec(memory_space=pltpu.SMEM)] + [whole] * (len(sums) + len(params))
    in_specs += [pl.BlockSpec(memory_space=pl.ANY)] if late else []
    return pl.pallas_call(
        functools.partial(scan_kernel, late),
        out_shape=[jax.ShapeDtypeStruct((64, 1024), jnp.bfloat16)] * (2 * blocks)
        + [jax.ShapeDtypeStruct((4, 16, 64, 128), jnp.float32)],
        in_specs=in_specs,
        out_specs=[whole] * (2 * blocks) + [pl.BlockSpec(memory_space=pl.ANY)],
        scratch_shapes=[
            pltpu.VMEM((blocks, 16, 64, 128), jnp.float32),
            pltpu.SemaphoreType.DMA((blocks,)),
        ],
        input_output_aliases={len(operands) - 1: 2 * blocks} if late else {},
        compiler_params=pltpu.CompilerParams(vmem_limit_bytes=48 << 20),
        cost_estimate=pl.CostEstimate(flops=1 << 20, bytes_accessed=1 << 16, transcendentals=0),
    )(*operands)


def assemble_kernel(place, *refs):
    pieces, out = refs[:-1], refs[-1]
    values = [piece[...] for piece in pieces[2:]]
    values[:2] = [
        jnp.where(place[8] == 0, late[...], early) for late, early in zip(pieces[:2], values[:2])
    ]
    for k, value in enumerate(values):
        out[:, pl.ds(pl.multiple_of(place[k] * 1024, 1024), 1024)] = value


def assemble(place, pieces):
    whole = pl.BlockSpec(memory_space=pltpu.VMEM)
    return pl.pallas_call(
        assemble_kernel,
        out_shape=jax.ShapeDtypeStruct((64, 8192), jnp.bfloat16),
        in_specs=[pl.BlockSpec(memory_space=pltpu.SMEM)] + [whole] * 10,
        out_specs=whole,
        compiler_params=pltpu.CompilerParams(vmem_limit_bytes=16 << 20),
    )(place, *pieces)


def reorder_kernel(place, tokens, *outs):
    width = 256
    for part in range(4):
        for piece in range(8):
            start = pl.multiple_of(place[part * 8 + piece] * width, width)
            outs[part][:, piece * width : (piece + 1) * width] = tokens[:, pl.ds(start, width)]


def reorder_tokens(tokens, place):
    rows = tokens.shape[0]
    whole = pl.BlockSpec(memory_space=pltpu.VMEM)
    return pl.pallas_call(
        reorder_kernel,
        out_shape=[jax.ShapeDtypeStruct((rows, 2048), tokens.dtype)] * 4,
        in_specs=[pl.BlockSpec(memory_space=pltpu.SMEM), whole],
        out_specs=[whole] * 4,
        compiler_params=pltpu.CompilerParams(vmem_limit_bytes=16 << 20),
    )(place, tokens)


TILE = 768


def project_kernel(pairs, place, *refs):
    chunks, refs = refs[: 2 * pairs], refs[2 * pairs :]
    near, far, out = refs[:4], refs[4:9], refs[9]
    core, zh, y = place[0], place[2], place[3]
    mine = jnp.concatenate([ref[...] for ref in near], axis=0)
    across = jnp.where(pl.program_id(0) == 0, far[3][...], far[4][...])
    twin = jnp.concatenate([ref[...] for ref in far[:3]] + [across], axis=0)
    rhs = jnp.concatenate(
        [jnp.where(zh == 0, mine, twin), jnp.where(zh == 0, twin, mine)], axis=0
    )
    for p in range(pairs):
        lhs = jnp.concatenate([chunks[2 * p][...], chunks[2 * p + 1][...]], axis=0)
        partial = jnp.dot(lhs, rhs, preferred_element_type=jnp.float32)
        for half, at in ((0, core), (256, 1 - core)):
            rows = pl.ds(pl.multiple_of(p * 128 + at * 64, 64), 64)
            for d in range(4):
                low = half + 64 * d
                out[y ^ d, rows, :] = partial[low : low + 64].astype(jnp.bfloat16)


def project(place, chunks, panels):
    pairs = len(chunks) // 2
    width = panels[0].shape[1]
    whole = pl.BlockSpec((256, 2048), lambda j: (0, 0))
    column = pl.BlockSpec((256, TILE), lambda j: (0, j))
    single = pl.BlockSpec((256, TILE), lambda j: (0, 0))
    return pl.pallas_call(
        functools.partial(project_kernel, pairs),
        grid=(2,),
        out_shape=jax.ShapeDtypeStruct((4, 128 * pairs, width), jnp.bfloat16),
        in_specs=[pl.BlockSpec(memory_space=pltpu.SMEM)]
        + [whole] * len(chunks) + [column] * 7 + [single] * 2,
        out_specs=pl.BlockSpec((4, 128 * pairs, TILE), lambda j: (0, 0, j)),
        compiler_params=pltpu.CompilerParams(vmem_limit_bytes=60 << 20),
        cost_estimate=pl.CostEstimate(flops=1 << 20, bytes_accessed=1 << 16, transcendentals=0),
    )(place, *chunks, *panels)


def marker(value):
    anywhere = pl.BlockSpec(memory_space=pl.ANY)
    return pl.pallas_call(
        lambda given, same: None,
        out_shape=jax.ShapeDtypeStruct(value.shape, value.dtype),
        in_specs=[anywhere],
        out_specs=anywhere,
        input_output_aliases={0: 0},
        cost_estimate=pl.CostEstimate(flops=1 << 36, bytes_accessed=1 << 16, transcendentals=0),
    )(value)


def after(values, *others):
    flat, tree = jax.tree.flatten(values)
    held = lax.optimization_barrier(tuple(flat) + tuple(jax.tree.leaves(others)))
    return jax.tree.unflatten(tree, held[: len(flat)])


def swap(value, axis, distance):
    size = lax.axis_size(axis)
    return lax.ppermute(value, axis, [(i, i ^ distance) for i in range(size)])


def exchange(parts):
    return lax.all_to_all(parts, "y", split_axis=0, concat_axis=0, tiled=True)


def add_up(came):
    return jnp.sum(came.astype(jnp.float32), axis=0).astype(jnp.bfloat16)


def per_device(tokens, w_x, w_b, w_c, w_dt, conv_x, conv_b, conv_c, dt_bias, decay_rate, d_skip):
    y, x, zh, zl, core = (lax.axis_index(a) for a in AXES)
    panel = jnp.concatenate([w_x, w_b, w_c, jnp.pad(w_dt, ((0, 0), (0, 112)))], axis=1)
    twin = marker(swap(panel, "zh", 1))
    near = [panel] + [swap(panel, "x", d) for d in (1, 3, 2)]

    sources = x ^ jnp.asarray([0, 1, 3, 2])
    order = (
        (jnp.arange(4) ^ y)[:, None, None] * 8
        + jnp.arange(2)[None, :, None]
        + sources[None, None, :] * 2
    ).astype(jnp.int32).reshape(32)
    parts = reorder_tokens(after(tokens, panel), order)
    rows = [parts[0]] + [swap(parts[d], "y", d) for d in (1, 2, 3)]
    own = jnp.concatenate(rows, axis=0)
    own_other = swap(own, "c", 1)

    line = ("zh", "zl")
    own_sent, twin = after((own, twin), near)
    right1 = lax.ppermute(own_sent, line, [(i, (i + 1) % 8) for i in range(8)])
    left1 = lax.ppermute(own_sent, line, [(i, (i - 1) % 8) for i in range(8)])
    next_x, mirror_x = swap(twin, "x", 1), swap(twin, "x", 3)
    across = [swap(next_x[:, :TILE], "x", 3), swap(mirror_x[:, TILE:], "x", 1)]
    panels = near + [twin, next_x, mirror_x, *across]

    place = jnp.stack([core, zl, zh, y]).astype(jnp.int32)
    left1, right1 = after((left1, right1), panels)
    sides = [left1, swap(left1, "c", 1), right1, swap(right1, "c", 1)]
    parts = project(place, [own, own_other], panels)
    came_own = exchange(parts)
    parts = project(place, after(sides, parts), panels)
    came_sides = exchange(parts)

    left1, right1 = after((left1, right1), parts)
    right2 = lax.ppermute(right1, line, [(1, 2), (2, 3), (5, 6), (6, 7)])
    left2 = lax.ppermute(left1, line, [(1, 0), (2, 1), (5, 4), (6, 5)])
    second = jnp.where(zl < 2, left2, right2)
    pair = after([second, swap(second, "c", 1)], parts)
    parts = project(place, pair, panels)
    came_own, came_sides = after((came_own, came_sides), parts)
    came_second = exchange(parts)

    params = [
        jnp.concatenate([conv_x, conv_b, conv_c], axis=1),
        jnp.pad(dt_bias, (0, 112))[None],
        jnp.pad(decay_rate, (0, 112))[None],
        jnp.repeat(d_skip, 64)[None],
    ]
    sums = add_up(came_sides)
    swapped = lax.ppermute(
        jnp.where(zl == 3, sums[:128], sums[128:]), line, [(i, (i + 4) % 8) for i in (0, 3, 4, 7)]
    )
    *early, states = scan(place, [sums, came_own], params)

    def to(piece, distance, flip, origins=range(4)):
        pairs = [
            (2 * z + c, 2 * ((z + distance) % 4) + (c ^ flip)) for z in origins for c in range(2)
        ]
        return lax.ppermute(piece, ("zl", "c"), pairs)

    pieces = [to(early[2], 1, 0, range(3)), to(early[3], 1, 1, range(3))]
    pieces += [early[0], to(early[1], 0, 1)]
    came_second, pieces = after((came_second, pieces))
    *last, states = scan(place, [sums, came_second, swapped], params, states)
    pieces += [to(last[2], 2, 0), to(last[3], 2, 1), to(last[4], 3, 0), to(last[5], 3, 1)]
    pieces = [to(last[0], 1, 0, [3]), to(last[1], 1, 1, [3])] + pieces
    origin = zl + jnp.asarray([3, 3, 0, 0, 2, 2, 1, 1])
    columns = (origin % 4) * 2 + (core + jnp.asarray([0, 1] * 4)) % 2
    columns = jnp.concatenate([columns, zl[None]]).astype(jnp.int32)
    return (assemble(columns, pieces), states)


def solution(mesh):
    fine = Mesh(mesh.devices.reshape(4, 4, 2, 4, 2), AXES)
    fsdp, head = ("y", "x", "zh"), ("zl", "c")
    in_specs = (
        P(AXES, None),
        P(fsdp, head),
        P(fsdp, head),
        P(fsdp, head),
        P(fsdp, head),
        P(None, head),
        P(None, head),
        P(None, head),
        P(head),
        P(head),
        P(head),
    )
    out_specs = (P(AXES, None), P(fsdp, head, None, None))
    return jax.shard_map(
        per_device, mesh=fine, in_specs=in_specs, out_specs=out_specs, check_vma=False
    )
```

```python
import functools

import jax
import jax.numpy as jnp
from jax import lax
from jax.experimental import pallas as pl
from jax.experimental.pallas import tpu as pltpu
from jax.sharding import Mesh, PartitionSpec as P

AXES = ("y", "x", "zh", "zl", "c")


def shifted(value, rows):
    at = lax.broadcasted_iota(jnp.int32, value.shape, 0)
    return jnp.where(at >= rows, pltpu.roll(value, rows, 0), 0.0)


def scan_block(current, before, refs, core, same, other, states):
    taps, bias, rate, skip = refs
    width = taps.shape[1]
    ext = jnp.concatenate([before[:, :width], current[:, :width]], axis=0)
    total = taps[0:1, :] * ext[13:141]
    for k in (1, 2, 3):
        total = total + taps[k : k + 1, :] * ext[13 + k : 141 + k]
    values = (total / (1.0 + jnp.exp(-total))).astype(jnp.bfloat16)
    xs, bs, cs = values[:, :1024], values[:, 1024:1152], values[:, 1152:1280]

    raw = current[:, width:] + bias[...]
    step = jnp.maximum(raw, 0.0) + jnp.log1p(jnp.exp(-jnp.abs(raw)))
    cum = -rate[...] * step
    for rows in (1, 2, 4, 8, 16, 32, 64):
        cum = cum + shifted(cum, rows)
    cum_t, step_t = cum.T, step.T
    factor = step * jnp.exp(cum[127:128, :] - cum)
    scores = lax.dot_general(cs, bs, (((1,), (1,)), ((), ())), preferred_element_type=jnp.float32)
    lower = lax.broadcasted_iota(jnp.int32, (128, 128), 0) >= lax.broadcasted_iota(
        jnp.int32, (128, 128), 1
    )
    left = lax.broadcasted_iota(jnp.int32, (128, 128), 1) < 64
    for pair in range(8):
        lanes = slice(128 * pair, 128 * pair + 128)
        x_pair = xs[:, lanes]
        wide = x_pair.astype(jnp.float32)
        outs = []
        for h in (2 * pair, 2 * pair + 1):
            diff = cum[:, h : h + 1] - cum_t[h : h + 1, :]
            decay = jnp.exp(jnp.where(lower, diff, -1e30))
            weights = (scores * decay * step_t[h : h + 1, :]).astype(jnp.bfloat16)
            outs.append(jnp.dot(weights, x_pair, preferred_element_type=jnp.float32))
        out = jnp.where(left, outs[0], outs[1]) + skip[:, lanes] * wide
        out = out.astype(jnp.bfloat16)
        top, bottom = out[:64], out[64:]
        same[:, lanes] = jnp.where(core == 0, top, bottom)
        other[:, lanes] = jnp.where(core == 0, bottom, top)
        column = jnp.where(
            left, factor[:, 2 * pair : 2 * pair + 1], factor[:, 2 * pair + 1 : 2 * pair + 2]
        )
        carried = (wide * column).astype(jnp.bfloat16)
        state = lax.dot_general(
            carried, bs, (((0,), (0,)), ((), ())), preferred_element_type=jnp.float32
        )
        states[2 * pair] = state[:64]
        states[2 * pair + 1] = state[64:]


def scan_kernel(late, place, *refs):
    core, zl = place[0], place[1]
    sums, came, *refs = refs
    if late:
        came, (swapped, *refs) = [came, *refs[:3]], refs[3:]
        refs = refs[:4] + refs[5:]
    params, (*pieces, states, scratch, sems) = refs[:4], refs[4:]

    def whole(ref):
        return ref[...].astype(jnp.float32)

    def tail(value):
        return value[112:128]

    ahead, behind = (sums[k : k + 128].astype(jnp.float32) for k in (0, 128))
    total = sum(came[d][...].astype(jnp.float32) for d in range(4))
    total = total.astype(jnp.bfloat16).astype(jnp.float32)
    always = zl >= 0
    if late:
        first = whole(swapped)
        ahead = jnp.where(zl == 3, first, ahead)
        behind = jnp.where(zl == 0, first, behind)
        work = [
            (zl == 3, first, jnp.zeros_like(tail(first)), 0),
            (always, total, jnp.where(zl == 2, 0.0, tail(ahead)), lax.rem(zl + 2, 4)),
            (always, behind, jnp.where(zl == 1, 0.0, tail(total)), lax.rem(zl + 3, 4)),
        ]
    else:
        work = [
            (always, total, jnp.where(zl == 0, 0.0, tail(behind)), zl),
            (zl < 3, ahead, tail(total), lax.rem(zl + 1, 4)),
        ]

    def copy(k, block):
        return pltpu.make_async_copy(scratch.at[k], states.at[block], sems.at[k])

    for k, (needed, current, before, block) in enumerate(work):
        @pl.when(needed)
        def _(k=k, current=current, before=before, block=block):
            same, other = pieces[2 * k], pieces[2 * k + 1]
            scan_block(current, before, params, core, same, other, scratch.at[k])
            copy(k, block).start()

    for k, (needed, _, _, block) in enumerate(work):
        pl.when(needed)(lambda k=k, block=block: copy(k, block).wait())


def scan(place, sums, params, states=None):
    whole = pl.BlockSpec(memory_space=pltpu.VMEM)
    late = states is not None
    blocks = 3 if late else 2
    operands = [place, *sums, *params] + ([states] if late else [])
    in_specs = [pl.BlockSpec(memory_space=pltpu.SMEM)] + [whole] * (len(sums) + len(params))
    in_specs += [pl.BlockSpec(memory_space=pl.ANY)] if late else []
    return pl.pallas_call(
        functools.partial(scan_kernel, late),
        out_shape=[jax.ShapeDtypeStruct((64, 1024), jnp.bfloat16)] * (2 * blocks)
        + [jax.ShapeDtypeStruct((4, 16, 64, 128), jnp.float32)],
        in_specs=in_specs,
        out_specs=[whole] * (2 * blocks) + [pl.BlockSpec(memory_space=pl.ANY)],
        scratch_shapes=[
            pltpu.VMEM((blocks, 16, 64, 128), jnp.float32),
            pltpu.SemaphoreType.DMA((blocks,)),
        ],
        input_output_aliases={len(operands) - 1: 2 * blocks} if late else {},
        compiler_params=pltpu.CompilerParams(vmem_limit_bytes=48 << 20),
        cost_estimate=pl.CostEstimate(flops=1 << 20, bytes_accessed=1 << 16, transcendentals=0),
    )(*operands)


def assemble_kernel(place, *refs):
    pieces, out = refs[:-1], refs[-1]
    values = [piece[...] for piece in pieces[2:]]
    values[:2] = [
        jnp.where(place[8] == 0, late[...], early) for late, early in zip(pieces[:2], values[:2])
    ]
    for k, value in enumerate(values):
        out[:, pl.ds(pl.multiple_of(place[k] * 1024, 1024), 1024)] = value


def assemble(place, pieces):
    whole = pl.BlockSpec(memory_space=pltpu.VMEM)
    return pl.pallas_call(
        assemble_kernel,
        out_shape=jax.ShapeDtypeStruct((64, 8192), jnp.bfloat16),
        in_specs=[pl.BlockSpec(memory_space=pltpu.SMEM)] + [whole] * 10,
        out_specs=whole,
        compiler_params=pltpu.CompilerParams(vmem_limit_bytes=16 << 20),
    )(place, *pieces)


def reorder_kernel(place, tokens, *outs):
    width = 256
    for part in range(4):
        for piece in range(8):
            start = pl.multiple_of(place[part * 8 + piece] * width, width)
            outs[part][:, piece * width : (piece + 1) * width] = tokens[:, pl.ds(start, width)]


def reorder_tokens(tokens, place):
    rows = tokens.shape[0]
    whole = pl.BlockSpec(memory_space=pltpu.VMEM)
    return pl.pallas_call(
        reorder_kernel,
        out_shape=[jax.ShapeDtypeStruct((rows, 2048), tokens.dtype)] * 4,
        in_specs=[pl.BlockSpec(memory_space=pltpu.SMEM), whole],
        out_specs=[whole] * 4,
        compiler_params=pltpu.CompilerParams(vmem_limit_bytes=16 << 20),
    )(place, tokens)


TILE = 768


def project_kernel(pairs, together, place, *refs):
    chunks, refs = refs[: 2 * pairs], refs[2 * pairs :]
    near, far, outs = refs[:4], refs[4:9], refs[9:]
    core, zh, y = place[0], place[2], place[3]
    mine = jnp.concatenate([ref[...] for ref in near], axis=0)
    across = jnp.where(pl.program_id(0) == 0, far[3][...], far[4][...])
    twin = jnp.concatenate([ref[...] for ref in far[:3]] + [across], axis=0)
    rhs = jnp.concatenate(
        [jnp.where(zh == 0, mine, twin), jnp.where(zh == 0, twin, mine)], axis=0
    )
    for p in range(pairs):
        lhs = jnp.concatenate([chunks[2 * p][...], chunks[2 * p + 1][...]], axis=0)
        partial = jnp.dot(lhs, rhs, preferred_element_type=jnp.float32)
        for half, at in ((0, core), (256, 1 - core)):
            rows = pl.ds(pl.multiple_of(p * 128 + at * 64, 64), 64)
            for d in range(4):
                low = half + 64 * d
                if together:
                    outs[0][y ^ d, rows, :] = partial[low : low + 64].astype(jnp.bfloat16)
                else:
                    outs[d][rows, :] = partial[low : low + 64].astype(outs[d].dtype)


def project(place, chunks, panels, together):
    pairs = len(chunks) // 2
    width = panels[0].shape[1]
    whole = pl.BlockSpec((256, 2048), lambda j: (0, 0))
    column = pl.BlockSpec((256, TILE), lambda j: (0, j))
    single = pl.BlockSpec((256, TILE), lambda j: (0, 0))
    shape = (128 * pairs, width)
    if together:
        out_shape = jax.ShapeDtypeStruct((4, *shape), jnp.bfloat16)
        out_specs = pl.BlockSpec((4, 128 * pairs, TILE), lambda j: (0, 0, j))
    else:
        out_shape = [jax.ShapeDtypeStruct(shape, jnp.float32)]
        out_shape += [jax.ShapeDtypeStruct(shape, jnp.bfloat16)] * 3
        out_specs = [pl.BlockSpec((128 * pairs, TILE), lambda j: (0, j))] * 4
    return pl.pallas_call(
        functools.partial(project_kernel, pairs, together),
        grid=(2,),
        out_shape=out_shape,
        in_specs=[pl.BlockSpec(memory_space=pltpu.SMEM)]
        + [whole] * len(chunks) + [column] * 7 + [single] * 2,
        out_specs=out_specs,
        compiler_params=pltpu.CompilerParams(vmem_limit_bytes=60 << 20),
        cost_estimate=pl.CostEstimate(flops=1 << 20, bytes_accessed=1 << 16, transcendentals=0),
    )(place, *chunks, *panels)


def marker(value):
    anywhere = pl.BlockSpec(memory_space=pl.ANY)
    return pl.pallas_call(
        lambda given, same: None,
        out_shape=jax.ShapeDtypeStruct(value.shape, value.dtype),
        in_specs=[anywhere],
        out_specs=anywhere,
        input_output_aliases={0: 0},
        cost_estimate=pl.CostEstimate(flops=1 << 36, bytes_accessed=1 << 16, transcendentals=0),
    )(value)


def after(values, *others):
    flat, tree = jax.tree.flatten(values)
    held = lax.optimization_barrier(tuple(flat) + tuple(jax.tree.leaves(others)))
    return jax.tree.unflatten(tree, held[: len(flat)])


def swap(value, axis, distance):
    size = lax.axis_size(axis)
    return lax.ppermute(value, axis, [(i, i ^ distance) for i in range(size)])


def exchange(parts):
    return [parts[0]] + [swap(parts[d], "y", d) for d in (1, 2, 3)]


def exchange_all(parts):
    return lax.all_to_all(parts, "y", split_axis=0, concat_axis=0, tiled=True)


def add_up(came):
    return jnp.sum(came.astype(jnp.float32), axis=0).astype(jnp.bfloat16)


def per_device(tokens, w_x, w_b, w_c, w_dt, conv_x, conv_b, conv_c, dt_bias, decay_rate, d_skip):
    y, x, zh, zl, core = (lax.axis_index(a) for a in AXES)
    panel = jnp.concatenate([w_x, w_b, w_c, jnp.pad(w_dt, ((0, 0), (0, 112)))], axis=1)
    twin = marker(swap(panel, "zh", 1))
    near = [panel] + [swap(panel, "x", d) for d in (1, 3, 2)]

    sources = x ^ jnp.asarray([0, 1, 3, 2])
    order = (
        (jnp.arange(4) ^ y)[:, None, None] * 8
        + jnp.arange(2)[None, :, None]
        + sources[None, None, :] * 2
    ).astype(jnp.int32).reshape(32)
    parts = reorder_tokens(after(tokens, panel), order)
    rows = [parts[0]] + [swap(parts[d], "y", d) for d in (1, 2, 3)]
    own = jnp.concatenate(rows, axis=0)
    own_other = swap(own, "c", 1)

    line = ("zh", "zl")
    own_sent, twin = after((own, twin), near)
    right1 = lax.ppermute(own_sent, line, [(i, (i + 1) % 8) for i in range(8)])
    left1 = lax.ppermute(own_sent, line, [(i, (i - 1) % 8) for i in range(8)])
    next_x, mirror_x = swap(twin, "x", 1), swap(twin, "x", 3)
    across = [swap(next_x[:, :TILE], "x", 3), swap(mirror_x[:, TILE:], "x", 1)]
    panels = near + [twin, next_x, mirror_x, *across]

    place = jnp.stack([core, zl, zh, y]).astype(jnp.int32)
    left1, right1 = after((left1, right1), panels)
    sides = [left1, swap(left1, "c", 1), right1, swap(right1, "c", 1)]
    parts = project(place, [own, own_other], panels, True)
    came_own = exchange_all(parts)
    parts = project(place, after(sides, parts), panels, True)
    came_sides = exchange_all(parts)

    left1, right1 = after((left1, right1), parts)
    right2 = lax.ppermute(right1, line, [(1, 2), (2, 3), (5, 6), (6, 7)])
    left2 = lax.ppermute(left1, line, [(1, 0), (2, 1), (5, 4), (6, 5)])
    second = jnp.where(zl < 2, left2, right2)
    pair = after([second, swap(second, "c", 1)], parts)
    parts = project(place, pair, panels, False)
    came_own, came_sides = after((came_own, came_sides), parts)
    came_second = exchange(parts)

    params = [
        jnp.concatenate([conv_x, conv_b, conv_c], axis=1),
        jnp.pad(dt_bias, (0, 112))[None],
        jnp.pad(decay_rate, (0, 112))[None],
        jnp.repeat(d_skip, 64)[None],
    ]
    sums = add_up(came_sides)
    swapped = lax.ppermute(
        jnp.where(zl == 3, sums[:128], sums[128:]), line, [(i, (i + 4) % 8) for i in (0, 3, 4, 7)]
    )
    *early, states = scan(place, [sums, came_own], params)

    def to(piece, distance, flip, origins=range(4)):
        pairs = [
            (2 * z + c, 2 * ((z + distance) % 4) + (c ^ flip)) for z in origins for c in range(2)
        ]
        return lax.ppermute(piece, ("zl", "c"), pairs)

    *last, states = scan(place, [sums, *came_second, swapped], params, states)
    beyond = [to(last[2], 2, 0), to(last[3], 2, 1)]
    wrapped = [to(last[0], 1, 0, [3]), to(last[1], 1, 1, [3])]
    behind = [to(last[4], 3, 0), to(last[5], 3, 1)]
    early = after(early, beyond[0])
    ahead = [to(early[2], 1, 0, range(3)), to(early[3], 1, 1, range(3))]
    pieces = wrapped + ahead + [early[0], to(early[1], 0, 1)] + beyond + behind
    origin = zl + jnp.asarray([3, 3, 0, 0, 2, 2, 1, 1])
    columns = (origin % 4) * 2 + (core + jnp.asarray([0, 1] * 4)) % 2
    columns = jnp.concatenate([columns, zl[None]]).astype(jnp.int32)
    return (assemble(columns, pieces), states)


def solution(mesh):
    fine = Mesh(mesh.devices.reshape(4, 4, 2, 4, 2), AXES)
    fsdp, head = ("y", "x", "zh"), ("zl", "c")
    in_specs = (
        P(AXES, None),
        P(fsdp, head),
        P(fsdp, head),
        P(fsdp, head),
        P(fsdp, head),
        P(None, head),
        P(None, head),
        P(None, head),
        P(head),
        P(head),
        P(head),
    )
    out_specs = (P(AXES, None), P(fsdp, head, None, None))
    return jax.shard_map(
        per_device, mesh=fine, in_specs=in_specs, out_specs=out_specs, check_vma=False
    )
```

```python
import functools

import jax
import jax.numpy as jnp
from jax import lax
from jax.experimental import pallas as pl
from jax.experimental.pallas import tpu as pltpu
from jax.sharding import Mesh, PartitionSpec as P

AXES = ("y", "x", "zh", "zl", "c")


def shifted(value, rows):
    at = lax.broadcasted_iota(jnp.int32, value.shape, 0)
    return jnp.where(at >= rows, pltpu.roll(value, rows, 0), 0.0)


def scan_block(current, before, refs, core, same, other, states):
    taps, bias, rate, skip = refs
    width = taps.shape[1]
    ext = jnp.concatenate([before[:, :width], current[:, :width]], axis=0)
    total = taps[0:1, :] * ext[13:141]
    for k in (1, 2, 3):
        total = total + taps[k : k + 1, :] * ext[13 + k : 141 + k]
    values = (total / (1.0 + jnp.exp(-total))).astype(jnp.bfloat16)
    xs, bs, cs = values[:, :1024], values[:, 1024:1152], values[:, 1152:1280]

    raw = current[:, width:] + bias[...]
    step = jnp.maximum(raw, 0.0) + jnp.log1p(jnp.exp(-jnp.abs(raw)))
    cum = -rate[...] * step
    for rows in (1, 2, 4, 8, 16, 32, 64):
        cum = cum + shifted(cum, rows)
    cum_t, step_t = cum.T, step.T
    factor = step * jnp.exp(cum[127:128, :] - cum)
    scores = lax.dot_general(cs, bs, (((1,), (1,)), ((), ())), preferred_element_type=jnp.float32)
    lower = lax.broadcasted_iota(jnp.int32, (128, 128), 0) >= lax.broadcasted_iota(
        jnp.int32, (128, 128), 1
    )
    left = lax.broadcasted_iota(jnp.int32, (128, 128), 1) < 64
    for pair in range(8):
        lanes = slice(128 * pair, 128 * pair + 128)
        x_pair = xs[:, lanes]
        wide = x_pair.astype(jnp.float32)
        outs = []
        for h in (2 * pair, 2 * pair + 1):
            diff = cum[:, h : h + 1] - cum_t[h : h + 1, :]
            decay = jnp.exp(jnp.where(lower, diff, -1e30))
            weights = (scores * decay * step_t[h : h + 1, :]).astype(jnp.bfloat16)
            outs.append(jnp.dot(weights, x_pair, preferred_element_type=jnp.float32))
        out = jnp.where(left, outs[0], outs[1]) + skip[:, lanes] * wide
        out = out.astype(jnp.bfloat16)
        top, bottom = out[:64], out[64:]
        same[:, lanes] = jnp.where(core == 0, top, bottom)
        other[:, lanes] = jnp.where(core == 0, bottom, top)
        column = jnp.where(
            left, factor[:, 2 * pair : 2 * pair + 1], factor[:, 2 * pair + 1 : 2 * pair + 2]
        )
        carried = (wide * column).astype(jnp.bfloat16)
        state = lax.dot_general(
            carried, bs, (((0,), (0,)), ((), ())), preferred_element_type=jnp.float32
        )
        states[2 * pair] = state[:64]
        states[2 * pair + 1] = state[64:]


def scan_kernel(late, place, *refs):
    core, zl = place[0], place[1]
    sums, came, *refs = refs
    if late:
        came, (swapped, *refs) = [came, *refs[:3]], refs[3:]
        refs = refs[:4] + refs[5:]
    params, (*pieces, states, scratch, sems) = refs[:4], refs[4:]

    def whole(ref):
        return ref[...].astype(jnp.float32)

    def tail(value):
        return value[112:128]

    ahead, behind = (sums[k : k + 128].astype(jnp.float32) for k in (0, 128))
    total = sum(came[d][...].astype(jnp.float32) for d in range(4))
    total = total.astype(jnp.bfloat16).astype(jnp.float32)
    always = zl >= 0
    if late:
        first = whole(swapped)
        ahead = jnp.where(zl == 3, first, ahead)
        behind = jnp.where(zl == 0, first, behind)
        work = [
            (zl == 3, first, jnp.zeros_like(tail(first)), 0),
            (always, total, jnp.where(zl == 2, 0.0, tail(ahead)), lax.rem(zl + 2, 4)),
            (always, behind, jnp.where(zl == 1, 0.0, tail(total)), lax.rem(zl + 3, 4)),
        ]
    else:
        work = [
            (always, total, jnp.where(zl == 0, 0.0, tail(behind)), zl),
            (zl < 3, ahead, tail(total), lax.rem(zl + 1, 4)),
        ]

    def copy(k, block):
        return pltpu.make_async_copy(scratch.at[k], states.at[block], sems.at[k])

    for k, (needed, current, before, block) in enumerate(work):
        @pl.when(needed)
        def _(k=k, current=current, before=before, block=block):
            same, other = pieces[2 * k], pieces[2 * k + 1]
            scan_block(current, before, params, core, same, other, scratch.at[k])
            copy(k, block).start()

    for k, (needed, _, _, block) in enumerate(work):
        pl.when(needed)(lambda k=k, block=block: copy(k, block).wait())


def scan(place, sums, params, states=None):
    whole = pl.BlockSpec(memory_space=pltpu.VMEM)
    late = states is not None
    blocks = 3 if late else 2
    operands = [place, *sums, *params] + ([states] if late else [])
    in_specs = [pl.BlockSpec(memory_space=pltpu.SMEM)] + [whole] * (len(sums) + len(params))
    in_specs += [pl.BlockSpec(memory_space=pl.ANY)] if late else []
    return pl.pallas_call(
        functools.partial(scan_kernel, late),
        out_shape=[jax.ShapeDtypeStruct((64, 1024), jnp.bfloat16)] * (2 * blocks)
        + [jax.ShapeDtypeStruct((4, 16, 64, 128), jnp.float32)],
        in_specs=in_specs,
        out_specs=[whole] * (2 * blocks) + [pl.BlockSpec(memory_space=pl.ANY)],
        scratch_shapes=[
            pltpu.VMEM((blocks, 16, 64, 128), jnp.float32),
            pltpu.SemaphoreType.DMA((blocks,)),
        ],
        input_output_aliases={len(operands) - 1: 2 * blocks} if late else {},
        compiler_params=pltpu.CompilerParams(vmem_limit_bytes=48 << 20),
        cost_estimate=pl.CostEstimate(flops=1 << 20, bytes_accessed=1 << 16, transcendentals=0),
    )(*operands)


def assemble_kernel(place, *refs):
    pieces, out = refs[:-1], refs[-1]
    values = [piece[...] for piece in pieces[2:]]
    values[:2] = [
        jnp.where(place[8] == 0, late[...], early) for late, early in zip(pieces[:2], values[:2])
    ]
    for k, value in enumerate(values):
        out[:, pl.ds(pl.multiple_of(place[k] * 1024, 1024), 1024)] = value


def assemble(place, pieces):
    whole = pl.BlockSpec(memory_space=pltpu.VMEM)
    return pl.pallas_call(
        assemble_kernel,
        out_shape=jax.ShapeDtypeStruct((64, 8192), jnp.bfloat16),
        in_specs=[pl.BlockSpec(memory_space=pltpu.SMEM)] + [whole] * 10,
        out_specs=whole,
        compiler_params=pltpu.CompilerParams(vmem_limit_bytes=16 << 20),
    )(place, *pieces)


def reorder_kernel(place, tokens, *outs):
    width = 256
    for part in range(4):
        for piece in range(8):
            start = pl.multiple_of(place[part * 8 + piece] * width, width)
            outs[part][:, piece * width : (piece + 1) * width] = tokens[:, pl.ds(start, width)]


def reorder_tokens(tokens, place):
    rows = tokens.shape[0]
    whole = pl.BlockSpec(memory_space=pltpu.VMEM)
    return pl.pallas_call(
        reorder_kernel,
        out_shape=[jax.ShapeDtypeStruct((rows, 2048), tokens.dtype)] * 4,
        in_specs=[pl.BlockSpec(memory_space=pltpu.SMEM), whole],
        out_specs=[whole] * 4,
        compiler_params=pltpu.CompilerParams(vmem_limit_bytes=16 << 20),
    )(place, tokens)


TILE = 768


def project_kernel(pairs, together, place, *refs):
    chunks, refs = refs[: 2 * pairs], refs[2 * pairs :]
    near, far, outs = refs[:4], refs[4:9], refs[9:]
    core, zh, y = place[0], place[2], place[3]
    mine = jnp.concatenate([ref[...] for ref in near], axis=0)
    across = jnp.where(pl.program_id(0) == 0, far[3][...], far[4][...])
    twin = jnp.concatenate([ref[...] for ref in far[:3]] + [across], axis=0)
    rhs = jnp.concatenate(
        [jnp.where(zh == 0, mine, twin), jnp.where(zh == 0, twin, mine)], axis=0
    )
    for p in range(pairs):
        lhs = jnp.concatenate([chunks[2 * p][...], chunks[2 * p + 1][...]], axis=0)
        partial = jnp.dot(lhs, rhs, preferred_element_type=jnp.float32)
        for half, at in ((0, core), (256, 1 - core)):
            rows = pl.ds(pl.multiple_of(p * 128 + at * 64, 64), 64)
            for d in range(4):
                low = half + 64 * d
                if together:
                    outs[0][y ^ d, rows, :] = partial[low : low + 64].astype(jnp.bfloat16)
                else:
                    outs[d][rows, :] = partial[low : low + 64].astype(outs[d].dtype)


def project(place, chunks, panels, together):
    pairs = len(chunks) // 2
    width = panels[0].shape[1]
    whole = pl.BlockSpec((256, 2048), lambda j: (0, 0))
    column = pl.BlockSpec((256, TILE), lambda j: (0, j))
    single = pl.BlockSpec((256, TILE), lambda j: (0, 0))
    shape = (128 * pairs, width)
    if together:
        out_shape = jax.ShapeDtypeStruct((4, *shape), jnp.bfloat16)
        out_specs = pl.BlockSpec((4, 128 * pairs, TILE), lambda j: (0, 0, j))
    else:
        out_shape = [jax.ShapeDtypeStruct(shape, jnp.float32)]
        out_shape += [jax.ShapeDtypeStruct(shape, jnp.bfloat16)] * 3
        out_specs = [pl.BlockSpec((128 * pairs, TILE), lambda j: (0, j))] * 4
    return pl.pallas_call(
        functools.partial(project_kernel, pairs, together),
        grid=(2,),
        out_shape=out_shape,
        in_specs=[pl.BlockSpec(memory_space=pltpu.SMEM)]
        + [whole] * len(chunks) + [column] * 7 + [single] * 2,
        out_specs=out_specs,
        compiler_params=pltpu.CompilerParams(vmem_limit_bytes=60 << 20),
        cost_estimate=pl.CostEstimate(flops=1 << 20, bytes_accessed=1 << 16, transcendentals=0),
    )(place, *chunks, *panels)


def marker(value):
    anywhere = pl.BlockSpec(memory_space=pl.ANY)
    return pl.pallas_call(
        lambda given, same: None,
        out_shape=jax.ShapeDtypeStruct(value.shape, value.dtype),
        in_specs=[anywhere],
        out_specs=anywhere,
        input_output_aliases={0: 0},
        cost_estimate=pl.CostEstimate(flops=1 << 36, bytes_accessed=1 << 16, transcendentals=0),
    )(value)


def after(values, *others):
    flat, tree = jax.tree.flatten(values)
    held = lax.optimization_barrier(tuple(flat) + tuple(jax.tree.leaves(others)))
    return jax.tree.unflatten(tree, held[: len(flat)])


def swap(value, axis, distance):
    size = lax.axis_size(axis)
    return lax.ppermute(value, axis, [(i, i ^ distance) for i in range(size)])


def exchange(parts):
    return [parts[0]] + [swap(parts[d], "y", d) for d in (1, 2, 3)]


def exchange_all(parts):
    return lax.all_to_all(parts, "y", split_axis=0, concat_axis=0, tiled=True)


def add_up(came):
    return jnp.sum(came.astype(jnp.float32), axis=0).astype(jnp.bfloat16)


def per_device(tokens, w_x, w_b, w_c, w_dt, conv_x, conv_b, conv_c, dt_bias, decay_rate, d_skip):
    y, x, zh, zl, core = (lax.axis_index(a) for a in AXES)
    panel = jnp.concatenate([w_x, w_b, w_c, jnp.pad(w_dt, ((0, 0), (0, 112)))], axis=1)
    twin = marker(swap(panel, "zh", 1))
    near = [panel] + [swap(panel, "x", d) for d in (1, 3, 2)]

    sources = x ^ jnp.asarray([0, 1, 3, 2])
    order = (
        (jnp.arange(4) ^ y)[:, None, None] * 8
        + jnp.arange(2)[None, :, None]
        + sources[None, None, :] * 2
    ).astype(jnp.int32).reshape(32)
    parts = reorder_tokens(after(tokens, panel), order)
    rows = [parts[0]] + [swap(parts[d], "y", d) for d in (1, 2, 3)]
    own = jnp.concatenate(rows, axis=0)
    own_other = swap(own, "c", 1)

    line = ("zh", "zl")
    own_sent, twin = after((own, twin), near)
    right1 = lax.ppermute(own_sent, line, [(i, (i + 1) % 8) for i in range(8)])
    left1 = lax.ppermute(own_sent, line, [(i, (i - 1) % 8) for i in range(8)])
    next_x, mirror_x = swap(twin, "x", 1), swap(twin, "x", 3)
    across = [swap(next_x[:, :TILE], "x", 3), swap(mirror_x[:, TILE:], "x", 1)]
    panels = near + [twin, next_x, mirror_x, *across]

    place = jnp.stack([core, zl, zh, y]).astype(jnp.int32)
    parts = project(place, [own, own_other], panels, True)
    came_own = exchange_all(parts)
    left1, right1 = after((left1, right1), parts)
    sides = [left1, swap(left1, "c", 1), right1, swap(right1, "c", 1)]
    parts = project(place, after(sides, parts), panels, True)
    came_sides = exchange_all(parts)

    left1, right1 = after((left1, right1), parts)
    right2 = lax.ppermute(right1, line, [(1, 2), (2, 3), (5, 6), (6, 7)])
    left2 = lax.ppermute(left1, line, [(1, 0), (2, 1), (5, 4), (6, 5)])
    second = jnp.where(zl < 2, left2, right2)
    pair = after([second, swap(second, "c", 1)], parts)
    parts = project(place, pair, panels, False)
    came_own, came_sides = after((came_own, came_sides), parts)
    came_second = exchange(parts)

    params = [
        jnp.concatenate([conv_x, conv_b, conv_c], axis=1),
        jnp.pad(dt_bias, (0, 112))[None],
        jnp.pad(decay_rate, (0, 112))[None],
        jnp.repeat(d_skip, 64)[None],
    ]
    sums = add_up(came_sides)
    swapped = lax.ppermute(
        jnp.where(zl == 3, sums[:128], sums[128:]), line, [(i, (i + 4) % 8) for i in (0, 3, 4, 7)]
    )
    *early, states = scan(place, [sums, came_own], params)

    def to(piece, distance, flip, origins=range(4)):
        pairs = [
            (2 * z + c, 2 * ((z + distance) % 4) + (c ^ flip)) for z in origins for c in range(2)
        ]
        return lax.ppermute(piece, ("zl", "c"), pairs)

    *last, states = scan(place, [sums, *came_second, swapped], params, states)
    beyond = [to(last[2], 2, 0), to(last[3], 2, 1)]
    wrapped = [to(last[0], 1, 0, [3]), to(last[1], 1, 1, [3])]
    behind = [to(last[4], 3, 0), to(last[5], 3, 1)]
    early = after(early, beyond[0])
    ahead = [to(early[2], 1, 0, range(3)), to(early[3], 1, 1, range(3))]
    pieces = wrapped + ahead + [early[0], to(early[1], 0, 1)] + beyond + behind
    origin = zl + jnp.asarray([3, 3, 0, 0, 2, 2, 1, 1])
    columns = (origin % 4) * 2 + (core + jnp.asarray([0, 1] * 4)) % 2
    columns = jnp.concatenate([columns, zl[None]]).astype(jnp.int32)
    return (assemble(columns, pieces), states)


def solution(mesh):
    fine = Mesh(mesh.devices.reshape(4, 4, 2, 4, 2), AXES)
    fsdp, head = ("y", "x", "zh"), ("zl", "c")
    in_specs = (
        P(AXES, None),
        P(fsdp, head),
        P(fsdp, head),
        P(fsdp, head),
        P(fsdp, head),
        P(None, head),
        P(None, head),
        P(None, head),
        P(head),
        P(head),
        P(head),
    )
    out_specs = (P(AXES, None), P(fsdp, head, None, None))
    return jax.shard_map(
        per_device, mesh=fine, in_specs=in_specs, out_specs=out_specs, check_vma=False
    )
```
